32 devices in a mesh: tok: 4 (over y, core), voc: 8 (over z, x).
Axes of the slice: x: 2, y: 2, z: 4, core: 2. Of those that a mesh axis runs over, the one named last changes fastest.
Arguments:
- hidden: bfloat16 [1024, 2048], P('tok')
- panel: bfloat16 [2048, 8192], P(None, 'voc'), may hold values from -0.1875 to 0.1875
- in_proj: bfloat16 [2048, 64], replicated, may hold values from -0.125 to 0.125
- out_proj: bfloat16 [8192, 64], P('voc'), may hold values from -6 to 6
- targets: int32 [1024], P('tok'), may hold values from 0 to 8191
- keep: int32 [1024], P('tok'), may hold values 0 or 1
- span_ids: int32 [1024], P('tok'), may hold values from 0 to 127, as said below
- store: bfloat16 [8192, 4096], P(('tok', 'voc')), may hold values from -6 to 6
Outputs:
- hidden_grad: bfloat16 [1024, 2048], P('tok', 'voc')
- scores: float32 [128, 8192], P(None, ('tok', 'voc'))
The draws below stay inside these ranges and needn't reach their ends.
Inputs may be any that keep to these rules, and one draw needn't show every extreme that they name: `span_ids`: tokens k * 256 to (k + 1) * 256 - 1 hold exactly the spans k * 32 to (k + 1) * 32 - 1 in increasing order, each of one or more tokens.
All inputs are finite; a program needn't handle non-finite values. No bound on the sum of `keep` on one device may be relied on, other than what follows from the above.
Results may differ from the reference program's by a relative error of at most 0.018.
Values may be sent and summed in bfloat16 or wider, within the bound.
A program may use at most 64 MiB of HBM per device.

```python
import math
import jax
import jax.numpy as jnp
import numpy as np
from jax import lax

D = 2048
PANEL = 8192
RANK = 64
TOK_DEV = 256
SPAN_DEV = 32
TOKENS = 1024
SPANS = 128
STORE_ROWS = 8192


def draw_hidden(key, part):
    values = jax.random.normal(jax.random.fold_in(key, 11), (TOKENS, D), jnp.float32)
    values = jnp.clip(values, -6.0, 6.0)
    return values.astype(jnp.bfloat16)


def draw_span_ids(key, part):
    blocks = TOKENS // TOK_DEV
    raw = jax.random.randint(jax.random.fold_in(key, 21), (blocks, TOK_DEV - 1), 0, 1 << 20)
    order = jnp.arange(TOK_DEV - 1, dtype=jnp.int32)
    ranked = jnp.argsort(raw * TOK_DEV + order[None, :], axis=1)
    cuts = ranked[:, :SPAN_DEV - 1].astype(jnp.int32) + 1
    position = jnp.arange(TOK_DEV, dtype=jnp.int32)
    local = jnp.sum((position[None, :, None] >= cuts[:, None, :]).astype(jnp.int32), axis=2)
    start = jnp.arange(blocks, dtype=jnp.int32)[:, None] * SPAN_DEV
    return (local + start).reshape(-1).astype(jnp.int32)


def plant(entries, key, least, high):
    longest = entries.shape.index(max(entries.shape))
    spots = []
    for shift in (0, 1):
        where = [jax.random.randint(jax.random.fold_in(key, axis), (), 0, length) for axis, length in enumerate(entries.shape)]
        where[longest] = (where[longest] + shift) % entries.shape[longest]
        spots.append(tuple(where))
    return entries.at[spots[0]].set(least).at[spots[1]].set(high)


def with_spikes(entries, key, source, target, shards_of, factor):
    def block_of(axis_at):
        return (jnp.arange(entries.shape[axis_at]) // (entries.shape[axis_at] // shards_of)).reshape((-1,) + (1,) * (entries.ndim - 1 - axis_at))

    one_side = jax.random.permutation(key, shards_of)[block_of(target)]
    far = (block_of(target) + shards_of // 2) % shards_of
    return jnp.where((block_of(source) == one_side) | (block_of(source) == far), factor * entries, entries)


def steps_of(key, extent, pieces, least, high):
    loudness, own = 1.0, jax.random.fold_in(key, 6)
    for dim, shards_of in pieces:
        steps = jnp.exp(jax.random.uniform(jax.random.fold_in(own, dim), (shards_of,), jnp.float32, least / len(pieces), high / len(pieces)))
        loudness = loudness * jnp.repeat(steps, extent[dim] // shards_of).reshape([-1 if axis == dim else 1 for axis in range(len(extent))])
    return loudness


def cumulative_ranks(number_of, lean):
    weights = [(1 << 20) // math.isqrt(grade ** lean) + 1 for grade in range(1, number_of + 1)]
    deviation = 1 + sum(weights) // (1 << 30)
    return np.cumsum(np.array([max(1, weight // deviation) for weight in weights]))


def skewed_ids(rng, shape, count, lean):
    table = cumulative_ranks(count, lean)
    pick = jax.random.randint(jax.random.fold_in(rng, 1), shape, 0, int(table[count - 1]))
    grade = jnp.searchsorted(jnp.asarray(table, jnp.int32), pick, side="right")
    return jax.random.permutation(jax.random.fold_in(rng, 2), count)[grade].astype(jnp.int32)


def scatter_about(stream_key, extent, spread, reach, pieces=(), held_as=jnp.bfloat16):
    entries = jax.random.normal(stream_key, extent, jnp.float32) * spread
    if len(pieces) > 0:
        entries = steps_of(stream_key, extent, pieces, -0.22, 0.18) * entries
    return jnp.clip(entries, min=-reach, max=reach).astype(held_as)


def heavy_noise(stream_key, extent, scale, bound, split, heavy, kind=jnp.bfloat16):
    result = scale * jax.random.normal(stream_key, extent, jnp.float32)
    if split:
        result = result * steps_of(stream_key, extent, split, -0.22, 0.18)
    return jnp.clip(with_spikes(result, jax.random.fold_in(stream_key, 3), *heavy), -bound, bound).astype(kind)


def setup_inputs(seed: int = 0) -> dict:
    key_of = jax.random.split(jax.random.key(seed), 9)
    return {
        "hidden": draw_hidden(jax.random.fold_in(key_of[8], 71), 0),
        "panel": heavy_noise(key_of[1], (D, PANEL), D ** -0.5, 0.1875, ((1, 8),), (1, 0, 8, 2.0)),
        "in_proj": scatter_about(key_of[2], (D, RANK), D ** -0.5, 0.125),
        "out_proj": scatter_about(key_of[3], (PANEL, RANK), 1.0, 6.0, ((0, 8),)),
        "targets": plant(skewed_ids(key_of[4], (TOKENS,), PANEL, 2), jax.random.fold_in(key_of[4], 3), 0, PANEL - 1).astype(jnp.int32),
        "keep": plant((jax.random.randint(key_of[5], (TOKENS,), 0, 4) < 3).astype(jnp.int32), jax.random.fold_in(key_of[5], 1), 0, 1),
        "span_ids": draw_span_ids(jax.random.fold_in(key_of[8], 71), 0),
        "store": scatter_about(key_of[7], (STORE_ROWS, RANK * RANK), 1.0, 6.0, ((0, 32),)),
    }


def reference(hidden, panel, in_proj, out_proj, targets, keep, span_ids, store):
    logits = jnp.dot(hidden, panel, preferred_element_type=jnp.float32)
    top = jnp.max(logits, axis=1)
    total = jnp.sum(jnp.exp(logits - top[:, None]), axis=1)
    lse = top + jnp.log(total)
    columns = jnp.arange(PANEL, dtype=jnp.int32)
    onehot = (targets[:, None] == columns[None, :]).astype(jnp.float32)
    grad = ((jnp.exp(logits - lse[:, None]) - onehot) * keep.astype(jnp.float32)[:, None]).astype(jnp.bfloat16)
    hidden_grad = lax.dot_general(grad, panel, (((1,), (1,)), ((), ())), preferred_element_type=jnp.float32).astype(jnp.bfloat16)
    inner = jnp.dot(hidden, in_proj, preferred_element_type=jnp.float32)
    outer = jnp.dot(grad, out_proj, preferred_element_type=jnp.float32)
    product = (inner[:, :, None] * outer[:, None, :]).reshape(inner.shape[0], RANK * RANK)
    queries = jax.ops.segment_sum(product, span_ids, num_segments=SPANS).astype(jnp.bfloat16)
    scores = lax.dot_general(queries, store, (((1,), (1,)), ((), ())), preferred_element_type=jnp.float32) / RANK
    return hidden_grad, scores
```

```python
import functools

import jax
import jax.numpy as jnp
from jax import lax
from jax.experimental import pallas as pl
from jax.experimental.pallas import tpu as pltpu
from jax.sharding import PartitionSpec as P

SPAN_DEV = 32
LANES = 128
ROWS16 = 16
PAIR = 2
MESH_ID = pl.DeviceIdType.MESH


def span_sums(member, inner, outer):
    weighted = member[:, :, None] * inner[None, :, :]
    summed = lax.dot_general(
        weighted,
        outer,
        (((1,), (0,)), ((), ())),
        precision=lax.Precision.HIGHEST,
        preferred_element_type=jnp.float32,
    )
    return summed.reshape(member.shape[0], inner.shape[1] * outer.shape[1])


def plain_body(hidden, panel, in_proj, out_proj, targets, keep, span_ids, store):
    panel_cols = panel.shape[1]
    logits = jnp.dot(hidden, panel, preferred_element_type=jnp.float32)
    local_top = jnp.max(logits, axis=1)
    top = lax.pmax(local_top, "voc")
    total = lax.psum(jnp.sum(jnp.exp(logits - top[:, None]), axis=1), "voc")
    lse = top + jnp.log(total)
    columns = lax.axis_index("voc") * panel_cols + jnp.arange(panel_cols, dtype=jnp.int32)
    onehot = (targets[:, None] == columns[None, :]).astype(jnp.float32)
    grad = ((jnp.exp(logits - lse[:, None]) - onehot) * keep.astype(jnp.float32)[:, None]).astype(
        jnp.bfloat16
    )
    partial_hidden = lax.dot_general(
        grad, panel, (((1,), (1,)), ((), ())), preferred_element_type=jnp.float32
    )
    hidden_grad = lax.psum_scatter(
        partial_hidden.astype(jnp.bfloat16), "voc", scatter_dimension=1, tiled=True
    )
    inner = jnp.dot(hidden, in_proj, preferred_element_type=jnp.float32)
    outer_part = jnp.dot(grad, out_proj, preferred_element_type=jnp.float32)
    local_span = span_ids - lax.axis_index("tok") * SPAN_DEV
    member = (local_span[None, :] == jnp.arange(SPAN_DEV, dtype=jnp.int32)[:, None]).astype(
        jnp.float32
    )
    outer = lax.psum(outer_part.astype(jnp.bfloat16), "voc").astype(jnp.float32)
    queries = span_sums(member, inner, outer).astype(jnp.bfloat16)
    scores = (
        lax.dot_general(
            lax.all_gather(queries, "tok", axis=0, tiled=True),
            store,
            (((1,), (1,)), ((), ())),
            preferred_element_type=jnp.float32,
        )
        / in_proj.shape[1]
    )
    return (hidden_grad, scores)


def dot_nt(a, b):
    return lax.dot_general(a, b, (((1,), (1,)), ((), ())), preferred_element_type=jnp.float32)


def fused_kernel(
    n_tok,
    n_voc,
    chunks,
    hidden_hbm,
    panel_hbm,
    inp_hbm,
    outp_hbm,
    targets_ref,
    keep_ref,
    span_ref,
    store_hbm,
    hg_ref,
    scores_ref,
    hidden,
    panel,
    inp,
    outp,
    store,
    logits,
    colstat,
    both,
    prod,
    stat,
    early,
    opart,
    rs,
    oall,
    weights,
    queries,
    xsrc,
    xdst,
    zsrc,
    zdst,
    load_sem,
    panel_sem,
    stat_s,
    stat_r,
    early_s,
    early_r,
    rs_s,
    rs_r,
    ag_s,
    ag_r,
    late_s,
    late_r,
    x_s,
    x_r,
    z_s,
    z_r,
):
    tok, dim = hidden.shape
    cols = panel.shape[1]
    rank = inp.shape[1]
    out_cols = dim // n_voc
    nz = n_voc // PAIR
    halves = tok // LANES
    i = lax.axis_index("tok")
    v = lax.axis_index("voc")
    z, x = v // PAIR, v % PAIR
    vpeers = [lax.rem(v + k, n_voc) for k in range(1, n_voc)]
    tpeers = [lax.rem(i + k, n_tok) for k in range(1, n_tok)]
    partner = z * PAIR + (PAIR - 1 - x)

    def remote(src, dst, ss, rs_, t, w):
        return pltpu.make_async_remote_copy(
            src_ref=src,
            dst_ref=dst,
            send_sem=ss,
            recv_sem=rs_,
            device_id=(t, w),
            device_id_type=MESH_ID,
        )

    barrier = pltpu.get_barrier_semaphore()
    for w in vpeers:
        pl.semaphore_signal(barrier, inc=1, device_id=(i, w), device_id_type=MESH_ID)
    for t in tpeers:
        pl.semaphore_signal(barrier, inc=1, device_id=(t, v), device_id_type=MESH_ID)

    width = cols // chunks
    load_hidden = pltpu.make_async_copy(hidden_hbm, hidden, load_sem.at[0])
    load_hidden.start()
    load_inp = pltpu.make_async_copy(inp_hbm, inp, load_sem.at[1])
    load_inp.start()
    load_panel = []
    for c in range(chunks):
        piece = pl.ds(c * width, width)
        load_panel.append(
            pltpu.make_async_copy(panel_hbm.at[:, piece], panel.at[:, piece], panel_sem.at[c])
        )
        load_panel[-1].start()
    load_outp = pltpu.make_async_copy(outp_hbm, outp, load_sem.at[2])
    load_outp.start()
    load_store = pltpu.make_async_copy(store_hbm, store, load_sem.at[3])
    load_store.start()

    target_col = jnp.broadcast_to(targets_ref[...].astype(jnp.float32), (LANES, tok)).T
    keep_row = keep_ref[...].astype(jnp.float32)
    keep_col = jnp.broadcast_to(keep_row, (LANES, tok)).T
    first = (v * cols).astype(jnp.float32)
    colstat[1] = target_col - first
    colstat[2] = keep_col

    load_hidden.wait()
    load_inp.wait()
    inner = jnp.dot(hidden[...], inp[...], preferred_element_type=jnp.float32)
    early[i, 0:rank, :] = inner.T.astype(jnp.bfloat16)
    local_span = (span_ref[...] - i * SPAN_DEV).astype(jnp.float32)
    early[i, rank : rank + ROWS16, :] = jnp.broadcast_to(local_span, (ROWS16, tok)).astype(
        jnp.bfloat16
    )

    for c in range(chunks):
        load_panel[c].wait()
        piece = pl.ds(c * width, width)
        logits[:, piece] = jnp.dot(hidden[...], panel[:, piece], preferred_element_type=jnp.float32)

    step = 32
    lane = lax.broadcasted_iota(jnp.int32, (step, LANES), 1)
    number = lax.broadcasted_iota(jnp.int32, (step, cols), 1).astype(jnp.float32)

    @pl.loop(0, tok // step)
    def _(r):
        at = pl.ds(pl.multiple_of(r * step, step), step)
        l = logits[at, :]
        m = jnp.max(l, axis=1, keepdims=True)
        e = jnp.exp(l - m)
        s = jnp.sum(e, axis=1, keepdims=True)
        colstat[0, at, :] = jnp.where(lane == 0, m, s)
        both[at, :] = e.astype(jnp.bfloat16)
        hit = number == colstat[1, at, 0:1]
        lower = pl.ds(pl.multiple_of(tok + r * step, step), step)
        both[lower, :] = jnp.where(hit, colstat[2, at, 0:1], 0.0).astype(jnp.bfloat16)

    mine = colstat[0].T[0:8, :]
    stat[v] = mine

    pl.semaphore_wait(barrier, n_voc + n_tok - 2)
    sends = []

    def send(copy):
        copy.start()
        sends.append(copy)

    for k, w in enumerate(vpeers):
        send(remote(stat.at[v], stat.at[v], stat_s.at[k], stat_r.at[v], i, w))
    for k, t in enumerate(tpeers):
        send(remote(early.at[i], early.at[i], early_s.at[k], early_r.at[i], t, v))

    load_outp.wait()
    outer2 = jnp.dot(both[...], outp[...], preferred_element_type=jnp.float32)

    @pl.loop(0, n_voc)
    def _(d):
        at = pl.ds(pl.multiple_of(d * out_cols, out_cols), out_cols)
        prod[d] = dot_nt(both[...], panel[at, :])

    for k, w in enumerate(vpeers):
        remote(stat.at[v], stat.at[w], stat_s.at[k], stat_r.at[w], i, w).wait_recv()
    tops = [stat[w, 0:1, :] for w in range(n_voc)]
    top = functools.reduce(jnp.maximum, tops)
    total = functools.reduce(
        jnp.add, [stat[w, 1:2, :] * jnp.exp(tops[w] - top) for w in range(n_voc)]
    )
    lse = top + jnp.log(total)
    factor = keep_row * jnp.exp(mine[0:1, :] - lse)
    colstat[3] = jnp.broadcast_to(factor, (LANES, tok)).T
    factor_col = colstat[3, :, 0:1]

    outer_t = (factor_col * outer2[:tok] - outer2[tok:]).T.astype(jnp.bfloat16)
    for j in range(n_voc):
        a, h = j // halves, j % halves
        opart[j] = outer_t[a * ROWS16 : (a + 1) * ROWS16, h * LANES : (h + 1) * LANES]
    for k, w in enumerate(vpeers):
        send(remote(opart.at[w], rs.at[v], rs_s.at[k], rs_r.at[v], i, w))

    def part_of(d):
        return factor_col * prod[d, 0:tok, :] - prod[d, tok : 2 * tok, :]

    order = [lax.rem(z + k, nz) for k in list(range(1, nz)) + [0]]
    for k, zz in enumerate(order):
        xsrc[k] = part_of(zz * PAIR + (PAIR - 1 - x)).astype(jnp.bfloat16)
        send(remote(xsrc.at[k], xdst.at[k], x_s.at[k], x_r.at[k], i, partner))

    for k, w in enumerate(vpeers):
        remote(opart.at[w], rs.at[w], rs_s.at[k], rs_r.at[w], i, w).wait_recv()
    rs[v] = opart[v]
    outer_mine = functools.reduce(jnp.add, [rs[w].astype(jnp.float32) for w in range(n_voc)])
    oall[i, v] = outer_mine.astype(jnp.bfloat16)
    for k, w in enumerate(vpeers):
        send(remote(oall.at[i, v], oall.at[i, v], ag_s.at[k], ag_r.at[v], i, w))

    def pass_on(k):
        zz = order[k]
        remote(xsrc.at[k], xdst.at[k], x_s.at[k], x_r.at[k], i, partner).wait_recv()
        total_k = part_of(zz * PAIR + x) + xdst[k].astype(jnp.float32)
        if k == nz - 1:
            return total_k
        zsrc[k] = total_k.astype(jnp.bfloat16)
        send(remote(zsrc.at[k], zdst.at[z], z_s.at[k], z_r.at[z], i, zz * PAIR + x))

    pass_on(0)
    for k, w in enumerate(vpeers):
        remote(oall.at[i, v], oall.at[i, w], ag_s.at[k], ag_r.at[w], i, w).wait_recv()
    for k, t in enumerate(tpeers):
        send(remote(oall.at[i], oall.at[i], late_s.at[k], late_r.at[i], t, v))
    for k in range(1, nz - 1):
        pass_on(k)

    for k, t in enumerate(tpeers):
        remote(early.at[i], early.at[t], early_s.at[k], early_r.at[t], t, v).wait_recv()
    span_no = lax.broadcasted_iota(jnp.int32, (SPAN_DEV, tok), 0).astype(jnp.float32)

    @pl.loop(0, n_tok)
    def _(b):
        ids = early[b, rank : rank + ROWS16, :].astype(jnp.float32)[0:1]
        member = (span_no == ids).astype(jnp.float32)
        inner_t = early[b, 0:rank, :].astype(jnp.float32)
        for a in range(rank):
            weights[b, a * SPAN_DEV : (a + 1) * SPAN_DEV, :] = (
                member * inner_t[a : a + 1, :]
            ).astype(jnp.bfloat16)

    kept = pass_on(nz - 1)
    hold = prod.at[0, 0:tok, :]
    hold[...] = kept

    for k, t in enumerate(tpeers):
        remote(oall.at[i], oall.at[t], late_s.at[k], late_r.at[t], t, v).wait_recv()
    low = lax.broadcasted_iota(jnp.int32, (SPAN_DEV, LANES), 1) < rank

    @pl.loop(0, n_tok)
    def _(b):
        rows = []
        for a in range(rank // ROWS16):
            rows.append(
                jnp.concatenate([oall[b, a * halves + h] for h in range(halves)], axis=1)
            )
        outer_b = jnp.concatenate(rows * (LANES // rank), axis=0)
        sums = dot_nt(weights[b], outer_b)
        at = pl.ds(pl.multiple_of(b * SPAN_DEV, SPAN_DEV), SPAN_DEV)
        for a in range(0, rank, 2):
            even = sums[a * SPAN_DEV : (a + 1) * SPAN_DEV]
            odd = sums[(a + 1) * SPAN_DEV : (a + 2) * SPAN_DEV]
            queries[at, a * rank : (a + 2) * rank] = jnp.where(low, even, odd).astype(
                jnp.bfloat16
            )

    load_store.wait()
    scores_ref[...] = dot_nt(queries[...], store[...]) / rank

    for k in range(1, nz):
        w = lax.rem(z + k, nz)
        remote(zsrc.at[0], zdst.at[w], z_s.at[0], z_r.at[w], i, w * PAIR + x).wait_recv()
    zdst[z] = jnp.zeros_like(zdst[z])
    hg_ref[...] = (
        hold[...]
        + functools.reduce(jnp.add, [zdst[w].astype(jnp.float32) for w in range(nz)])
    ).astype(jnp.bfloat16)
    for copy in sends:
        copy.wait_send()


def fused_fits(n_tok, n_voc, hidden, panel, in_proj):
    tok, dim = hidden.shape
    rank = in_proj.shape[1]
    return (
        n_voc % PAIR == 0
        and n_tok > 1
        and (rank // ROWS16) * (tok // LANES) == n_voc
        and rank * 2 == LANES
        and dim % (n_voc * LANES) == 0
        and panel.shape[1] % (2 * LANES) == 0
        and SPAN_DEV % ROWS16 == 0
    )


def body(n_tok, n_voc, hidden, panel, in_proj, out_proj, targets, keep, span_ids, store):
    if not fused_fits(n_tok, n_voc, hidden, panel, in_proj):
        return plain_body(hidden, panel, in_proj, out_proj, targets, keep, span_ids, store)
    tok, dim = hidden.shape
    cols = panel.shape[1]
    rank = in_proj.shape[1]
    out_cols = dim // n_voc
    nz = n_voc // PAIR
    chunks = cols // (2 * LANES)
    bf, f32 = jnp.bfloat16, jnp.float32
    block = (nz, tok, out_cols)
    dma = pltpu.SemaphoreType.DMA
    anywhere = pl.BlockSpec(memory_space=pl.ANY)
    vmem = pl.BlockSpec(memory_space=pltpu.VMEM)
    return pl.pallas_call(
        functools.partial(fused_kernel, n_tok, n_voc, chunks),
        out_shape=(
            jax.ShapeDtypeStruct((tok, out_cols), bf),
            jax.ShapeDtypeStruct((n_tok * SPAN_DEV, store.shape[0]), f32),
        ),
        in_specs=[anywhere] * 4 + [vmem] * 3 + [anywhere],
        out_specs=(vmem, vmem),
        scratch_shapes=[
            pltpu.VMEM(hidden.shape, bf),
            pltpu.VMEM(panel.shape, bf),
            pltpu.VMEM(in_proj.shape, bf),
            pltpu.VMEM(out_proj.shape, bf),
            pltpu.VMEM(store.shape, bf),
            pltpu.VMEM((tok, cols), f32),
            pltpu.VMEM((4, tok, LANES), f32),
            pltpu.VMEM((2 * tok, cols), bf),
            pltpu.VMEM((n_voc, 2 * tok, out_cols), f32),
            pltpu.VMEM((n_voc, 8, tok), f32),
            pltpu.VMEM((n_tok, rank + ROWS16, tok), bf),
            pltpu.VMEM((n_voc, ROWS16, LANES), bf),
            pltpu.VMEM((n_voc, ROWS16, LANES), bf),
            pltpu.VMEM((n_tok, n_voc, ROWS16, LANES), bf),
            pltpu.VMEM((n_tok, rank * SPAN_DEV, tok), bf),
            pltpu.VMEM((n_tok * SPAN_DEV, rank * rank), bf),
            pltpu.VMEM(block, bf),
            pltpu.VMEM(block, bf),
            pltpu.VMEM(block, bf),
            pltpu.VMEM(block, bf),
            dma((4,)),
            dma((chunks,)),
            dma((n_voc,)),
            dma((n_voc,)),
            dma((n_tok,)),
            dma((n_tok,)),
            dma((n_voc,)),
            dma((n_voc,)),
            dma((n_voc,)),
            dma((n_voc,)),
            dma((n_tok,)),
            dma((n_tok,)),
            dma((nz,)),
            dma((nz,)),
            dma((nz,)),
            dma((nz,)),
        ],
        compiler_params=pltpu.CompilerParams(
            collective_id=0, has_side_effects=True, vmem_limit_bytes=44 * 1024 * 1024
        ),
    )(
        hidden,
        panel,
        in_proj,
        out_proj,
        targets.reshape(1, tok),
        keep.reshape(1, tok),
        span_ids.reshape(1, tok),
        store,
    )


def solution(mesh):
    placed = (
        P("tok", None),
        P(None, "voc"),
        P(),
        P("voc", None),
        P("tok"),
        P("tok"),
        P("tok"),
        P(("tok", "voc"), None),
    )
    return jax.shard_map(
        functools.partial(body, mesh.shape["tok"], mesh.shape["voc"]),
        mesh=mesh,
        in_specs=placed,
        out_specs=(P("tok", "voc"), P(None, ("tok", "voc"))),
        check_vma=False,
    )
```

```python
import functools

import jax
import jax.numpy as jnp
from jax import lax
from jax.experimental import pallas as pl
from jax.experimental.pallas import tpu as pltpu
from jax.sharding import PartitionSpec as P

SPAN_DEV = 32
LANES = 128
ROWS16 = 16
PAIR = 2
MESH_ID = pl.DeviceIdType.MESH


def span_sums(member, inner, outer):
    weighted = member[:, :, None] * inner[None, :, :]
    summed = lax.dot_general(
        weighted,
        outer,
        (((1,), (0,)), ((), ())),
        precision=lax.Precision.HIGHEST,
        preferred_element_type=jnp.float32,
    )
    return summed.reshape(member.shape[0], inner.shape[1] * outer.shape[1])


def plain_body(hidden, panel, in_proj, out_proj, targets, keep, span_ids, store):
    panel_cols = panel.shape[1]
    logits = jnp.dot(hidden, panel, preferred_element_type=jnp.float32)
    local_top = jnp.max(logits, axis=1)
    top = lax.pmax(local_top, "voc")
    total = lax.psum(jnp.sum(jnp.exp(logits - top[:, None]), axis=1), "voc")
    lse = top + jnp.log(total)
    columns = lax.axis_index("voc") * panel_cols + jnp.arange(panel_cols, dtype=jnp.int32)
    onehot = (targets[:, None] == columns[None, :]).astype(jnp.float32)
    grad = ((jnp.exp(logits - lse[:, None]) - onehot) * keep.astype(jnp.float32)[:, None]).astype(
        jnp.bfloat16
    )
    partial_hidden = lax.dot_general(
        grad, panel, (((1,), (1,)), ((), ())), preferred_element_type=jnp.float32
    )
    hidden_grad = lax.psum_scatter(
        partial_hidden.astype(jnp.bfloat16), "voc", scatter_dimension=1, tiled=True
    )
    inner = jnp.dot(hidden, in_proj, preferred_element_type=jnp.float32)
    outer_part = jnp.dot(grad, out_proj, preferred_element_type=jnp.float32)
    local_span = span_ids - lax.axis_index("tok") * SPAN_DEV
    member = (local_span[None, :] == jnp.arange(SPAN_DEV, dtype=jnp.int32)[:, None]).astype(
        jnp.float32
    )
    outer = lax.psum(outer_part.astype(jnp.bfloat16), "voc").astype(jnp.float32)
    queries = span_sums(member, inner, outer).astype(jnp.bfloat16)
    scores = (
        lax.dot_general(
            lax.all_gather(queries, "tok", axis=0, tiled=True),
            store,
            (((1,), (1,)), ((), ())),
            preferred_element_type=jnp.float32,
        )
        / in_proj.shape[1]
    )
    return (hidden_grad, scores)


def dot_nt(a, b):
    return lax.dot_general(a, b, (((1,), (1,)), ((), ())), preferred_element_type=jnp.float32)


def fused_kernel(
    n_tok,
    n_voc,
    chunks,
    hidden_hbm,
    panel_hbm,
    inp_hbm,
    outp_hbm,
    targets_hbm,
    keep_hbm,
    span_hbm,
    store_hbm,
    hg_ref,
    scores_ref,
    hidden,
    panel,
    inp,
    outp,
    store,
    ids_ref,
    logits,
    colstat,
    both,
    prod,
    stat,
    early,
    opart,
    rs,
    oall,
    weights,
    queries,
    xsrc,
    xdst,
    zsrc,
    zdst,
    load_sem,
    panel_sem,
    stat_s,
    stat_r,
    early_s,
    early_r,
    rs_s,
    rs_r,
    ag_s,
    ag_r,
    late_s,
    late_r,
    x_s,
    x_r,
    z_s,
    z_r,
):
    tok, dim = hidden.shape
    cols = panel.shape[1]
    rank = inp.shape[0]
    out_cols = dim // n_voc
    nz = n_voc // PAIR
    halves = tok // LANES
    i = lax.axis_index("tok")
    v = lax.axis_index("voc")
    z, x = v // PAIR, v % PAIR
    vpeers = [lax.rem(v + k, n_voc) for k in range(1, n_voc)]
    tpeers = [lax.rem(i + k, n_tok) for k in range(1, n_tok)]
    partner = z * PAIR + (PAIR - 1 - x)

    def remote(src, dst, ss, rs_, t, w):
        return pltpu.make_async_remote_copy(
            src_ref=src,
            dst_ref=dst,
            send_sem=ss,
            recv_sem=rs_,
            device_id=(t, w),
            device_id_type=MESH_ID,
        )

    barrier = pltpu.get_barrier_semaphore()
    for w in vpeers:
        pl.semaphore_signal(barrier, inc=1, device_id=(i, w), device_id_type=MESH_ID)
    for t in tpeers:
        pl.semaphore_signal(barrier, inc=1, device_id=(t, v), device_id_type=MESH_ID)

    width = cols // chunks
    loads = []
    for k, ref in enumerate((targets_hbm, keep_hbm, span_hbm)):
        loads.append(pltpu.make_async_copy(ref, ids_ref.at[k], load_sem.at[4 + k]))
        loads[-1].start()
    load_hidden = pltpu.make_async_copy(hidden_hbm, hidden, load_sem.at[0])
    load_hidden.start()
    load_inp = pltpu.make_async_copy(inp_hbm, inp, load_sem.at[1])
    load_inp.start()
    load_panel = []
    for c in range(chunks):
        piece = pl.ds(c * width, width)
        load_panel.append(
            pltpu.make_async_copy(panel_hbm.at[:, piece], panel.at[:, piece], panel_sem.at[c])
        )
        load_panel[-1].start()
    load_outp = pltpu.make_async_copy(outp_hbm, outp, load_sem.at[2])
    load_outp.start()
    load_store = pltpu.make_async_copy(store_hbm, store, load_sem.at[3])
    load_store.start()

    for copy in loads:
        copy.wait()
    target_col = jnp.broadcast_to(ids_ref[0].astype(jnp.float32), (LANES, tok)).T
    keep_row = ids_ref[1].astype(jnp.float32)
    keep_col = jnp.broadcast_to(keep_row, (LANES, tok)).T
    first = (v * cols).astype(jnp.float32)
    colstat[1] = target_col - first
    colstat[2] = keep_col

    load_hidden.wait()
    load_inp.wait()
    early[i, 0:rank, :] = dot_nt(inp[...], hidden[...]).astype(jnp.bfloat16)
    local_span = (ids_ref[2] - i * SPAN_DEV).astype(jnp.float32)
    early[i, rank : rank + ROWS16, :] = jnp.broadcast_to(local_span, (ROWS16, tok)).astype(
        jnp.bfloat16
    )

    for c in range(chunks):
        load_panel[c].wait()
        piece = pl.ds(c * width, width)
        logits[:, piece] = jnp.dot(hidden[...], panel[:, piece], preferred_element_type=jnp.float32)

    step = 32
    lane = lax.broadcasted_iota(jnp.int32, (step, LANES), 1)
    number = lax.broadcasted_iota(jnp.int32, (step, cols), 1).astype(jnp.float32)

    @pl.loop(0, tok // step)
    def _(r):
        at = pl.ds(pl.multiple_of(r * step, step), step)
        l = logits[at, :]
        m = jnp.max(l, axis=1, keepdims=True)
        e = jnp.exp(l - m)
        s = jnp.sum(e, axis=1, keepdims=True)
        colstat[0, at, :] = jnp.where(lane == 0, m, s)
        both[at, :] = e.astype(jnp.bfloat16)
        hit = number == colstat[1, at, 0:1]
        lower = pl.ds(pl.multiple_of(tok + r * step, step), step)
        both[lower, :] = jnp.where(hit, colstat[2, at, 0:1], 0.0).astype(jnp.bfloat16)

    mine = colstat[0].T[0:8, :]
    stat[v] = mine

    pl.semaphore_wait(barrier, n_voc + n_tok - 2)
    sends = []

    def send(copy):
        copy.start()
        sends.append(copy)

    for k, w in enumerate(vpeers):
        send(remote(stat.at[v], stat.at[v], stat_s.at[k], stat_r.at[v], i, w))
    for k, t in enumerate(tpeers):
        send(remote(early.at[i], early.at[i], early_s.at[k], early_r.at[i], t, v))

    load_outp.wait()
    outer2 = dot_nt(outp[...], both[...])

    @pl.loop(0, n_voc)
    def _(d):
        at = pl.ds(pl.multiple_of(d * out_cols, out_cols), out_cols)
        prod[d] = dot_nt(both[...], panel[at, :])

    for k, w in enumerate(vpeers):
        remote(stat.at[v], stat.at[w], stat_s.at[k], stat_r.at[w], i, w).wait_recv()
    tops = [stat[w, 0:1, :] for w in range(n_voc)]
    top = functools.reduce(jnp.maximum, tops)
    total = functools.reduce(
        jnp.add, [stat[w, 1:2, :] * jnp.exp(tops[w] - top) for w in range(n_voc)]
    )
    lse = top + jnp.log(total)
    factor = keep_row * jnp.exp(mine[0:1, :] - lse)
    colstat[3] = jnp.broadcast_to(factor, (LANES, tok)).T
    factor_col = colstat[3, :, 0:1]

    outer_t = (factor * outer2[:, :tok] - outer2[:, tok:]).astype(jnp.bfloat16)
    for j in range(n_voc):
        a, h = j // halves, j % halves
        opart[j] = outer_t[a * ROWS16 : (a + 1) * ROWS16, h * LANES : (h + 1) * LANES]
    for k, w in enumerate(vpeers):
        send(remote(opart.at[w], rs.at[v], rs_s.at[k], rs_r.at[v], i, w))

    def part_of(d):
        return factor_col * prod[d, 0:tok, :] - prod[d, tok : 2 * tok, :]

    shifts = [nz // 2] + [k for k in range(1, nz) if k != nz // 2] + [0]
    order = [lax.rem(z + k, nz) for k in shifts]

    def send_x(k):
        xsrc[k] = part_of(order[k] * PAIR + (PAIR - 1 - x)).astype(jnp.bfloat16)
        send(remote(xsrc.at[k], xdst.at[k], x_s.at[k], x_r.at[k], i, partner))

    def pass_on(k):
        zz = order[k]
        remote(xsrc.at[k], xdst.at[k], x_s.at[k], x_r.at[k], i, partner).wait_recv()
        total_k = part_of(zz * PAIR + x) + xdst[k].astype(jnp.float32)
        if k == nz - 1:
            return total_k
        zsrc[k] = total_k.astype(jnp.bfloat16)
        send(remote(zsrc.at[k], zdst.at[z], z_s.at[k], z_r.at[z], i, zz * PAIR + x))

    send_x(0)
    for k, t in enumerate(tpeers):
        remote(early.at[i], early.at[t], early_s.at[k], early_r.at[t], t, v).wait_recv()
    span_no = lax.broadcasted_iota(jnp.int32, (SPAN_DEV, tok), 0).astype(jnp.float32)

    @pl.loop(0, n_tok)
    def _(b):
        ids = early[b, rank : rank + ROWS16, :].astype(jnp.float32)[0:1]
        member = (span_no == ids).astype(jnp.float32)
        inner_t = early[b, 0:rank, :].astype(jnp.float32)
        for a in range(rank):
            weights[b, a * SPAN_DEV : (a + 1) * SPAN_DEV, :] = (
                member * inner_t[a : a + 1, :]
            ).astype(jnp.bfloat16)

    for k, w in enumerate(vpeers):
        remote(opart.at[w], rs.at[w], rs_s.at[k], rs_r.at[w], i, w).wait_recv()
    rs[v] = opart[v]
    outer_mine = functools.reduce(jnp.add, [rs[w].astype(jnp.float32) for w in range(n_voc)])
    oall[i, v] = outer_mine.astype(jnp.bfloat16)
    for k, w in enumerate(vpeers):
        send(remote(oall.at[i, v], oall.at[i, v], ag_s.at[k], ag_r.at[v], i, w))
    for k in range(1, nz):
        send_x(k)
    pass_on(0)

    for k, w in enumerate(vpeers):
        remote(oall.at[i, v], oall.at[i, w], ag_s.at[k], ag_r.at[w], i, w).wait_recv()
    for k, t in enumerate(tpeers):
        send(remote(oall.at[i], oall.at[i], late_s.at[k], late_r.at[i], t, v))
    pass_on(1)

    for k, t in enumerate(tpeers):
        remote(oall.at[i], oall.at[t], late_s.at[k], late_r.at[t], t, v).wait_recv()
    low = lax.broadcasted_iota(jnp.int32, (SPAN_DEV, LANES), 1) < rank

    @pl.loop(0, n_tok)
    def _(b):
        rows = []
        for a in range(rank // ROWS16):
            rows.append(
                jnp.concatenate([oall[b, a * halves + h] for h in range(halves)], axis=1)
            )
        outer_b = jnp.concatenate(rows * (LANES // rank), axis=0)
        sums = dot_nt(weights[b], outer_b)
        at = pl.ds(pl.multiple_of(b * SPAN_DEV, SPAN_DEV), SPAN_DEV)
        for a in range(0, rank, 2):
            even = sums[a * SPAN_DEV : (a + 1) * SPAN_DEV]
            odd = sums[(a + 1) * SPAN_DEV : (a + 2) * SPAN_DEV]
            queries[at, a * rank : (a + 2) * rank] = jnp.where(low, even, odd).astype(
                jnp.bfloat16
            )

    for k in range(2, nz - 1):
        pass_on(k)
    load_store.wait()
    scores_ref[...] = dot_nt(queries[...], store[...]) / rank

    kept = pass_on(nz - 1)
    for k in range(1, nz):
        w = lax.rem(z + k, nz)
        remote(zsrc.at[0], zdst.at[w], z_s.at[0], z_r.at[w], i, w * PAIR + x).wait_recv()
    zdst[z] = jnp.zeros_like(zdst[z])
    hg_ref[...] = (
        kept
        + functools.reduce(jnp.add, [zdst[w].astype(jnp.float32) for w in range(nz)])
    ).astype(jnp.bfloat16)
    for copy in sends:
        copy.wait_send()


def fused_fits(n_tok, n_voc, hidden, panel, in_proj):
    tok, dim = hidden.shape
    rank = in_proj.shape[1]
    return (
        n_voc % PAIR == 0
        and n_voc // PAIR > 2
        and n_tok > 1
        and (rank // ROWS16) * (tok // LANES) == n_voc
        and rank * 2 == LANES
        and dim % (n_voc * LANES) == 0
        and panel.shape[1] % (2 * LANES) == 0
        and SPAN_DEV % ROWS16 == 0
    )


def body(n_tok, n_voc, hidden, panel, in_proj, out_proj, targets, keep, span_ids, store):
    if not fused_fits(n_tok, n_voc, hidden, panel, in_proj):
        return plain_body(hidden, panel, in_proj, out_proj, targets, keep, span_ids, store)
    tok, dim = hidden.shape
    cols = panel.shape[1]
    rank = in_proj.shape[1]
    out_cols = dim // n_voc
    nz = n_voc // PAIR
    chunks = cols // (2 * LANES)
    bf, f32 = jnp.bfloat16, jnp.float32
    block = (nz, tok, out_cols)
    dma = pltpu.SemaphoreType.DMA
    anywhere = pl.BlockSpec(memory_space=pltpu.HBM)
    vmem = pl.BlockSpec(memory_space=pltpu.VMEM)
    return pl.pallas_call(
        functools.partial(fused_kernel, n_tok, n_voc, chunks),
        out_shape=(
            jax.ShapeDtypeStruct((tok, out_cols), bf),
            jax.ShapeDtypeStruct((n_tok * SPAN_DEV, store.shape[0]), f32),
        ),
        in_specs=[anywhere] * 8,
        out_specs=(vmem, vmem),
        scratch_shapes=[
            pltpu.VMEM(hidden.shape, bf),
            pltpu.VMEM(panel.shape, bf),
            pltpu.VMEM((rank, dim), bf),
            pltpu.VMEM((rank, cols), bf),
            pltpu.VMEM(store.shape, bf),
            pltpu.VMEM((3, 1, tok), jnp.int32),
            pltpu.VMEM((tok, cols), f32),
            pltpu.VMEM((4, tok, LANES), f32),
            pltpu.VMEM((2 * tok, cols), bf),
            pltpu.VMEM((n_voc, 2 * tok, out_cols), f32),
            pltpu.VMEM((n_voc, 8, tok), f32),
            pltpu.VMEM((n_tok, rank + ROWS16, tok), bf),
            pltpu.VMEM((n_voc, ROWS16, LANES), bf),
            pltpu.VMEM((n_voc, ROWS16, LANES), bf),
            pltpu.VMEM((n_tok, n_voc, ROWS16, LANES), bf),
            pltpu.VMEM((n_tok, rank * SPAN_DEV, tok), bf),
            pltpu.VMEM((n_tok * SPAN_DEV, rank * rank), bf),
            pltpu.VMEM(block, bf),
            pltpu.VMEM(block, bf),
            pltpu.VMEM(block, bf),
            pltpu.VMEM(block, bf),
            dma((7,)),
            dma((chunks,)),
            dma((n_voc,)),
            dma((n_voc,)),
            dma((n_tok,)),
            dma((n_tok,)),
            dma((n_voc,)),
            dma((n_voc,)),
            dma((n_voc,)),
            dma((n_voc,)),
            dma((n_tok,)),
            dma((n_tok,)),
            dma((nz,)),
            dma((nz,)),
            dma((nz,)),
            dma((nz,)),
        ],
        compiler_params=pltpu.CompilerParams(
            collective_id=0, has_side_effects=True, vmem_limit_bytes=60 * 1024 * 1024
        ),
    )(
        hidden,
        panel,
        in_proj.T,
        out_proj.T,
        targets.reshape(1, tok),
        keep.reshape(1, tok),
        span_ids.reshape(1, tok),
        store,
    )


def solution(mesh):
    placed = (
        P("tok", None),
        P(None, "voc"),
        P(),
        P("voc", None),
        P("tok"),
        P("tok"),
        P("tok"),
        P(("tok", "voc"), None),
    )
    return jax.shard_map(
        functools.partial(body, mesh.shape["tok"], mesh.shape["voc"]),
        mesh=mesh,
        in_specs=placed,
        out_specs=(P("tok", "voc"), P(None, ("tok", "voc"))),
        check_vma=False,
    )
```

```python
import functools

import jax
import jax.numpy as jnp
from jax import lax
from jax.experimental import pallas as pl
from jax.experimental.pallas import tpu as pltpu
from jax.sharding import PartitionSpec as P

SPAN_DEV = 32
LANES = 128
ROWS16 = 16
PAIR = 2
MESH_ID = pl.DeviceIdType.MESH


def span_sums(member, inner, outer):
    weighted = member[:, :, None] * inner[None, :, :]
    summed = lax.dot_general(
        weighted,
        outer,
        (((1,), (0,)), ((), ())),
        precision=lax.Precision.HIGHEST,
        preferred_element_type=jnp.float32,
    )
    return summed.reshape(member.shape[0], inner.shape[1] * outer.shape[1])


def plain_body(hidden, panel, in_proj, out_proj, targets, keep, span_ids, store):
    panel_cols = panel.shape[1]
    logits = jnp.dot(hidden, panel, preferred_element_type=jnp.float32)
    local_top = jnp.max(logits, axis=1)
    top = lax.pmax(local_top, "voc")
    total = lax.psum(jnp.sum(jnp.exp(logits - top[:, None]), axis=1), "voc")
    lse = top + jnp.log(total)
    columns = lax.axis_index("voc") * panel_cols + jnp.arange(panel_cols, dtype=jnp.int32)
    onehot = (targets[:, None] == columns[None, :]).astype(jnp.float32)
    grad = ((jnp.exp(logits - lse[:, None]) - onehot) * keep.astype(jnp.float32)[:, None]).astype(
        jnp.bfloat16
    )
    partial_hidden = lax.dot_general(
        grad, panel, (((1,), (1,)), ((), ())), preferred_element_type=jnp.float32
    )
    hidden_grad = lax.psum_scatter(
        partial_hidden.astype(jnp.bfloat16), "voc", scatter_dimension=1, tiled=True
    )
    inner = jnp.dot(hidden, in_proj, preferred_element_type=jnp.float32)
    outer_part = jnp.dot(grad, out_proj, preferred_element_type=jnp.float32)
    local_span = span_ids - lax.axis_index("tok") * SPAN_DEV
    member = (local_span[None, :] == jnp.arange(SPAN_DEV, dtype=jnp.int32)[:, None]).astype(
        jnp.float32
    )
    outer = lax.psum(outer_part.astype(jnp.bfloat16), "voc").astype(jnp.float32)
    queries = span_sums(member, inner, outer).astype(jnp.bfloat16)
    scores = (
        lax.dot_general(
            lax.all_gather(queries, "tok", axis=0, tiled=True),
            store,
            (((1,), (1,)), ((), ())),
            preferred_element_type=jnp.float32,
        )
        / in_proj.shape[1]
    )
    return (hidden_grad, scores)


def dot_nt(a, b):
    return lax.dot_general(a, b, (((1,), (1,)), ((), ())), preferred_element_type=jnp.float32)


def fused_kernel(
    n_tok,
    n_voc,
    chunks,
    hidden_hbm,
    panel_hbm,
    inp_hbm,
    outp_hbm,
    targets_hbm,
    keep_hbm,
    span_hbm,
    store_hbm,
    hg_ref,
    scores_ref,
    hidden,
    panel,
    inp,
    outp,
    store,
    ids_ref,
    logits,
    colstat,
    both,
    prod,
    stat,
    early,
    opart,
    rs,
    oall,
    weights,
    queries,
    xsrc,
    xdst,
    zsrc,
    zdst,
    load_sem,
    panel_sem,
    stat_s,
    stat_r,
    early_s,
    early_r,
    rs_s,
    rs_r,
    ag_s,
    ag_r,
    late_s,
    late_r,
    x_s,
    x_r,
    z_s,
    z_r,
):
    tok, dim = hidden.shape
    cols = panel.shape[1]
    rank = inp.shape[0]
    out_cols = dim // n_voc
    nz = n_voc // PAIR
    halves = tok // LANES
    i = lax.axis_index("tok")
    v = lax.axis_index("voc")
    z, x = v // PAIR, v % PAIR
    vpeers = [lax.rem(v + k, n_voc) for k in range(1, n_voc)]
    tpeers = [lax.rem(i + k, n_tok) for k in range(1, n_tok)]
    partner = z * PAIR + (PAIR - 1 - x)

    def remote(src, dst, ss, rs_, t, w):
        return pltpu.make_async_remote_copy(
            src_ref=src,
            dst_ref=dst,
            send_sem=ss,
            recv_sem=rs_,
            device_id=(t, w),
            device_id_type=MESH_ID,
        )

    barrier = pltpu.get_barrier_semaphore()
    for w in vpeers:
        pl.semaphore_signal(barrier, inc=1, device_id=(i, w), device_id_type=MESH_ID)
    for t in tpeers:
        pl.semaphore_signal(barrier, inc=1, device_id=(t, v), device_id_type=MESH_ID)

    width = cols // chunks
    loads = []
    for k, ref in enumerate((targets_hbm, keep_hbm, span_hbm)):
        loads.append(pltpu.make_async_copy(ref, ids_ref.at[k], load_sem.at[4 + k]))
        loads[-1].start()
    load_hidden = pltpu.make_async_copy(hidden_hbm, hidden, load_sem.at[0])
    load_hidden.start()
    load_inp = pltpu.make_async_copy(inp_hbm, inp, load_sem.at[1])
    load_inp.start()
    load_panel = []
    for c in range(chunks):
        piece = pl.ds(c * width, width)
        load_panel.append(
            pltpu.make_async_copy(panel_hbm.at[:, piece], panel.at[:, piece], panel_sem.at[c])
        )
        load_panel[-1].start()
    load_outp = pltpu.make_async_copy(outp_hbm, outp, load_sem.at[2])
    load_outp.start()
    load_store = pltpu.make_async_copy(store_hbm, store, load_sem.at[3])
    load_store.start()

    for copy in loads:
        copy.wait()
    target_col = jnp.broadcast_to(ids_ref[0].astype(jnp.float32), (LANES, tok)).T
    keep_row = ids_ref[1].astype(jnp.float32)
    keep_col = jnp.broadcast_to(keep_row, (LANES, tok)).T
    first = (v * cols).astype(jnp.float32)
    colstat[1] = target_col - first
    colstat[2] = keep_col

    load_hidden.wait()
    load_inp.wait()
    early[i, 0:rank, :] = dot_nt(inp[...], hidden[...]).astype(jnp.bfloat16)
    local_span = (ids_ref[2] - i * SPAN_DEV).astype(jnp.float32)
    early[i, rank : rank + ROWS16, :] = jnp.broadcast_to(local_span, (ROWS16, tok)).astype(
        jnp.bfloat16
    )

    for c in range(chunks):
        load_panel[c].wait()
        piece = pl.ds(c * width, width)
        logits[:, piece] = jnp.dot(hidden[...], panel[:, piece], preferred_element_type=jnp.float32)

    step = 32
    lane = lax.broadcasted_iota(jnp.int32, (step, LANES), 1)
    number = lax.broadcasted_iota(jnp.int32, (step, cols), 1).astype(jnp.float32)

    @pl.loop(0, tok // step)
    def _(r):
        at = pl.ds(pl.multiple_of(r * step, step), step)
        l = logits[at, :]
        m = jnp.max(l, axis=1, keepdims=True)
        e = jnp.exp(l - m)
        s = jnp.sum(e, axis=1, keepdims=True)
        colstat[0, at, :] = jnp.where(lane == 0, m, s)
        both[at, :] = e.astype(jnp.bfloat16)
        hit = number == colstat[1, at, 0:1]
        lower = pl.ds(pl.multiple_of(tok + r * step, step), step)
        both[lower, :] = jnp.where(hit, colstat[2, at, 0:1], 0.0).astype(jnp.bfloat16)

    mine = colstat[0].T[0:8, :]
    stat[v] = mine

    pl.semaphore_wait(barrier, n_voc + n_tok - 2)
    sends = []

    def send(copy):
        copy.start()
        sends.append(copy)

    for k, w in enumerate(vpeers):
        send(remote(stat.at[v], stat.at[v], stat_s.at[k], stat_r.at[v], i, w))
    for k, t in enumerate(tpeers):
        send(remote(early.at[i], early.at[i], early_s.at[k], early_r.at[i], t, v))

    load_outp.wait()
    outer2 = dot_nt(outp[...], both[...])

    def products(side):
        @pl.loop(0, nz)
        def _(k):
            d = k * PAIR + side
            at = pl.ds(pl.multiple_of(d * out_cols, out_cols), out_cols)
            prod[d] = dot_nt(both[...], panel[at, :])

    products(PAIR - 1 - x)

    for k, w in enumerate(vpeers):
        remote(stat.at[v], stat.at[w], stat_s.at[k], stat_r.at[w], i, w).wait_recv()
    tops = [stat[w, 0:1, :] for w in range(n_voc)]
    top = functools.reduce(jnp.maximum, tops)
    total = functools.reduce(
        jnp.add, [stat[w, 1:2, :] * jnp.exp(tops[w] - top) for w in range(n_voc)]
    )
    lse = top + jnp.log(total)
    factor = keep_row * jnp.exp(mine[0:1, :] - lse)
    colstat[3] = jnp.broadcast_to(factor, (LANES, tok)).T
    factor_col = colstat[3, :, 0:1]

    outer_t = (factor * outer2[:, :tok] - outer2[:, tok:]).astype(jnp.bfloat16)
    for j in range(n_voc):
        a, h = j // halves, j % halves
        opart[j] = outer_t[a * ROWS16 : (a + 1) * ROWS16, h * LANES : (h + 1) * LANES]
    for k, w in enumerate(vpeers):
        send(remote(opart.at[w], rs.at[v], rs_s.at[k], rs_r.at[v], i, w))

    def part_of(d):
        return factor_col * prod[d, 0:tok, :] - prod[d, tok : 2 * tok, :]

    shifts = [nz // 2] + [k for k in range(1, nz) if k != nz // 2] + [0]
    order = [lax.rem(z + k, nz) for k in shifts]

    def send_x(k):
        xsrc[k] = part_of(order[k] * PAIR + (PAIR - 1 - x)).astype(jnp.bfloat16)
        send(remote(xsrc.at[k], xdst.at[k], x_s.at[k], x_r.at[k], i, partner))

    def pass_on(k):
        zz = order[k]
        remote(xsrc.at[k], xdst.at[k], x_s.at[k], x_r.at[k], i, partner).wait_recv()
        total_k = part_of(zz * PAIR + x) + xdst[k].astype(jnp.float32)
        if k == nz - 1:
            return total_k
        zsrc[k] = total_k.astype(jnp.bfloat16)
        send(remote(zsrc.at[k], zdst.at[z], z_s.at[k], z_r.at[z], i, zz * PAIR + x))

    send_x(0)
    for k, t in enumerate(tpeers):
        remote(early.at[i], early.at[t], early_s.at[k], early_r.at[t], t, v).wait_recv()
    span_no = lax.broadcasted_iota(jnp.int32, (SPAN_DEV, tok), 0).astype(jnp.float32)

    @pl.loop(0, n_tok)
    def _(b):
        ids = early[b, rank : rank + ROWS16, :].astype(jnp.float32)[0:1]
        member = (span_no == ids).astype(jnp.float32)
        inner_t = early[b, 0:rank, :].astype(jnp.float32)
        for a in range(rank):
            weights[b, a * SPAN_DEV : (a + 1) * SPAN_DEV, :] = (
                member * inner_t[a : a + 1, :]
            ).astype(jnp.bfloat16)

    for k, w in enumerate(vpeers):
        remote(opart.at[w], rs.at[w], rs_s.at[k], rs_r.at[w], i, w).wait_recv()
    rs[v] = opart[v]
    outer_mine = functools.reduce(jnp.add, [rs[w].astype(jnp.float32) for w in range(n_voc)])
    oall[i, v] = outer_mine.astype(jnp.bfloat16)
    for k, w in enumerate(vpeers):
        send(remote(oall.at[i, v], oall.at[i, v], ag_s.at[k], ag_r.at[v], i, w))
    for k in range(1, nz):
        send_x(k)
    products(x)
    pass_on(0)

    for k, w in enumerate(vpeers):
        remote(oall.at[i, v], oall.at[i, w], ag_s.at[k], ag_r.at[w], i, w).wait_recv()
    for k, t in enumerate(tpeers):
        send(remote(oall.at[i], oall.at[i], late_s.at[k], late_r.at[i], t, v))
    pass_on(1)

    for k, t in enumerate(tpeers):
        remote(oall.at[i], oall.at[t], late_s.at[k], late_r.at[t], t, v).wait_recv()
    low = lax.broadcasted_iota(jnp.int32, (SPAN_DEV, LANES), 1) < rank

    @pl.loop(0, n_tok)
    def _(b):
        rows = []
        for a in range(rank // ROWS16):
            rows.append(
                jnp.concatenate([oall[b, a * halves + h] for h in range(halves)], axis=1)
            )
        outer_b = jnp.concatenate(rows * (LANES // rank), axis=0)
        sums = dot_nt(weights[b], outer_b)
        at = pl.ds(pl.multiple_of(b * SPAN_DEV, SPAN_DEV), SPAN_DEV)
        for a in range(0, rank, 2):
            even = sums[a * SPAN_DEV : (a + 1) * SPAN_DEV]
            odd = sums[(a + 1) * SPAN_DEV : (a + 2) * SPAN_DEV]
            queries[at, a * rank : (a + 2) * rank] = jnp.where(low, even, odd).astype(
                jnp.bfloat16
            )

    for k in range(2, nz - 1):
        pass_on(k)
    load_store.wait()
    scores_ref[...] = dot_nt(queries[...], store[...]) / rank

    kept = pass_on(nz - 1)
    for k in range(1, nz):
        w = lax.rem(z + k, nz)
        remote(zsrc.at[0], zdst.at[w], z_s.at[0], z_r.at[w], i, w * PAIR + x).wait_recv()
    zdst[z] = jnp.zeros_like(zdst[z])
    hg_ref[...] = (
        kept
        + functools.reduce(jnp.add, [zdst[w].astype(jnp.float32) for w in range(nz)])
    ).astype(jnp.bfloat16)
    for copy in sends:
        copy.wait_send()


def fused_fits(n_tok, n_voc, hidden, panel, in_proj):
    tok, dim = hidden.shape
    rank = in_proj.shape[1]
    return (
        n_voc % PAIR == 0
        and n_voc // PAIR > 2
        and n_tok > 1
        and (rank // ROWS16) * (tok // LANES) == n_voc
        and rank * 2 == LANES
        and dim % (n_voc * LANES) == 0
        and panel.shape[1] % (2 * LANES) == 0
        and SPAN_DEV % ROWS16 == 0
    )


def body(n_tok, n_voc, hidden, panel, in_proj, out_proj, targets, keep, span_ids, store):
    if not fused_fits(n_tok, n_voc, hidden, panel, in_proj):
        return plain_body(hidden, panel, in_proj, out_proj, targets, keep, span_ids, store)
    tok, dim = hidden.shape
    cols = panel.shape[1]
    rank = in_proj.shape[1]
    out_cols = dim // n_voc
    nz = n_voc // PAIR
    chunks = cols // (2 * LANES)
    bf, f32 = jnp.bfloat16, jnp.float32
    block = (nz, tok, out_cols)
    dma = pltpu.SemaphoreType.DMA
    anywhere = pl.BlockSpec(memory_space=pltpu.HBM)
    vmem = pl.BlockSpec(memory_space=pltpu.VMEM)
    return pl.pallas_call(
        functools.partial(fused_kernel, n_tok, n_voc, chunks),
        out_shape=(
            jax.ShapeDtypeStruct((tok, out_cols), bf),
            jax.ShapeDtypeStruct((n_tok * SPAN_DEV, store.shape[0]), f32),
        ),
        in_specs=[anywhere] * 8,
        out_specs=(vmem, vmem),
        scratch_shapes=[
            pltpu.VMEM(hidden.shape, bf),
            pltpu.VMEM(panel.shape, bf),
            pltpu.VMEM((rank, dim), bf),
            pltpu.VMEM((rank, cols), bf),
            pltpu.VMEM(store.shape, bf),
            pltpu.VMEM((3, 1, tok), jnp.int32),
            pltpu.VMEM((tok, cols), f32),
            pltpu.VMEM((4, tok, LANES), f32),
            pltpu.VMEM((2 * tok, cols), bf),
            pltpu.VMEM((n_voc, 2 * tok, out_cols), f32),
            pltpu.VMEM((n_voc, 8, tok), f32),
            pltpu.VMEM((n_tok, rank + ROWS16, tok), bf),
            pltpu.VMEM((n_voc, ROWS16, LANES), bf),
            pltpu.VMEM((n_voc, ROWS16, LANES), bf),
            pltpu.VMEM((n_tok, n_voc, ROWS16, LANES), bf),
            pltpu.VMEM((n_tok, rank * SPAN_DEV, tok), bf),
            pltpu.VMEM((n_tok * SPAN_DEV, rank * rank), bf),
            pltpu.VMEM(block, bf),
            pltpu.VMEM(block, bf),
            pltpu.VMEM(block, bf),
            pltpu.VMEM(block, bf),
            dma((7,)),
            dma((chunks,)),
            dma((n_voc,)),
            dma((n_voc,)),
            dma((n_tok,)),
            dma((n_tok,)),
            dma((n_voc,)),
            dma((n_voc,)),
            dma((n_voc,)),
            dma((n_voc,)),
            dma((n_tok,)),
            dma((n_tok,)),
            dma((nz,)),
            dma((nz,)),
            dma((nz,)),
            dma((nz,)),
        ],
        compiler_params=pltpu.CompilerParams(
            collective_id=0, has_side_effects=True, vmem_limit_bytes=60 * 1024 * 1024
        ),
    )(
        hidden,
        panel,
        in_proj.T,
        out_proj.T,
        targets.reshape(1, tok),
        keep.reshape(1, tok),
        span_ids.reshape(1, tok),
        store,
    )


def solution(mesh):
    placed = (
        P("tok", None),
        P(None, "voc"),
        P(),
        P("voc", None),
        P("tok"),
        P("tok"),
        P("tok"),
        P(("tok", "voc"), None),
    )
    return jax.shard_map(
        functools.partial(body, mesh.shape["tok"], mesh.shape["voc"]),
        mesh=mesh,
        in_specs=placed,
        out_specs=(P("tok", "voc"), P(None, ("tok", "voc"))),
        check_vma=False,
    )
```

```python
import functools

import jax
import jax.numpy as jnp
from jax import lax
from jax.experimental import pallas as pl
from jax.experimental.pallas import tpu as pltpu
from jax.sharding import PartitionSpec as P

SPAN_DEV = 32
LANES = 128
ROWS16 = 16
PAIR = 2
MESH_ID = pl.DeviceIdType.MESH


def span_sums(member, inner, outer):
    weighted = member[:, :, None] * inner[None, :, :]
    summed = lax.dot_general(
        weighted,
        outer,
        (((1,), (0,)), ((), ())),
        precision=lax.Precision.HIGHEST,
        preferred_element_type=jnp.float32,
    )
    return summed.reshape(member.shape[0], inner.shape[1] * outer.shape[1])


def plain_body(hidden, panel, in_proj, out_proj, targets, keep, span_ids, store):
    panel_cols = panel.shape[1]
    logits = jnp.dot(hidden, panel, preferred_element_type=jnp.float32)
    local_top = jnp.max(logits, axis=1)
    top = lax.pmax(local_top, "voc")
    total = lax.psum(jnp.sum(jnp.exp(logits - top[:, None]), axis=1), "voc")
    lse = top + jnp.log(total)
    columns = lax.axis_index("voc") * panel_cols + jnp.arange(panel_cols, dtype=jnp.int32)
    onehot = (targets[:, None] == columns[None, :]).astype(jnp.float32)
    grad = ((jnp.exp(logits - lse[:, None]) - onehot) * keep.astype(jnp.float32)[:, None]).astype(
        jnp.bfloat16
    )
    partial_hidden = lax.dot_general(
        grad, panel, (((1,), (1,)), ((), ())), preferred_element_type=jnp.float32
    )
    hidden_grad = lax.psum_scatter(
        partial_hidden.astype(jnp.bfloat16), "voc", scatter_dimension=1, tiled=True
    )
    inner = jnp.dot(hidden, in_proj, preferred_element_type=jnp.float32)
    outer_part = jnp.dot(grad, out_proj, preferred_element_type=jnp.float32)
    local_span = span_ids - lax.axis_index("tok") * SPAN_DEV
    member = (local_span[None, :] == jnp.arange(SPAN_DEV, dtype=jnp.int32)[:, None]).astype(
        jnp.float32
    )
    outer = lax.psum(outer_part.astype(jnp.bfloat16), "voc").astype(jnp.float32)
    queries = span_sums(member, inner, outer).astype(jnp.bfloat16)
    scores = (
        lax.dot_general(
            lax.all_gather(queries, "tok", axis=0, tiled=True),
            store,
            (((1,), (1,)), ((), ())),
            preferred_element_type=jnp.float32,
        )
        / in_proj.shape[1]
    )
    return (hidden_grad, scores)


def dot_nt(a, b):
    return lax.dot_general(a, b, (((1,), (1,)), ((), ())), preferred_element_type=jnp.float32)


def fused_kernel(
    n_tok,
    n_voc,
    chunks,
    hidden_hbm,
    panel_hbm,
    inp_hbm,
    outp_hbm,
    ids_hbm,
    store_hbm,
    hg_ref,
    scores_ref,
    hidden,
    panel,
    inp,
    outp,
    store,
    ids_ref,
    logits,
    colstat,
    both,
    prod,
    stat,
    early,
    opart,
    rs,
    oall,
    weights,
    queries,
    xsrc,
    xdst,
    zsrc,
    zdst,
    load_sem,
    panel_sem,
    stat_s,
    stat_r,
    early_s,
    early_r,
    rs_s,
    rs_r,
    ag_s,
    ag_r,
    late_s,
    late_r,
    x_s,
    x_r,
    z_s,
    z_r,
):
    tok, dim = hidden.shape
    cols = panel.shape[1]
    rank = inp.shape[0]
    out_cols = dim // n_voc
    nz = n_voc // PAIR
    halves = tok // LANES
    i = lax.axis_index("tok")
    v = lax.axis_index("voc")
    z, x = v // PAIR, v % PAIR
    vpeers = [lax.rem(v + k, n_voc) for k in range(1, n_voc)]
    tpeers = [lax.rem(i + k, n_tok) for k in range(1, n_tok)]
    partner = z * PAIR + (PAIR - 1 - x)

    def remote(src, dst, ss, rs_, t, w):
        return pltpu.make_async_remote_copy(
            src_ref=src,
            dst_ref=dst,
            send_sem=ss,
            recv_sem=rs_,
            device_id=(t, w),
            device_id_type=MESH_ID,
        )

    barrier = pltpu.get_barrier_semaphore()
    for w in vpeers:
        pl.semaphore_signal(barrier, inc=1, device_id=(i, w), device_id_type=MESH_ID)
    for t in tpeers:
        pl.semaphore_signal(barrier, inc=1, device_id=(t, v), device_id_type=MESH_ID)

    width = cols // chunks
    load_ids = pltpu.make_async_copy(ids_hbm, ids_ref, load_sem.at[4])
    load_ids.start()
    load_hidden = pltpu.make_async_copy(hidden_hbm, hidden, load_sem.at[0])
    load_hidden.start()
    load_inp = pltpu.make_async_copy(inp_hbm, inp, load_sem.at[1])
    load_inp.start()
    load_panel = []
    for c in range(chunks):
        piece = pl.ds(c * width, width)
        load_panel.append(
            pltpu.make_async_copy(panel_hbm.at[:, piece], panel.at[:, piece], panel_sem.at[c])
        )
        load_panel[-1].start()
    load_outp = pltpu.make_async_copy(outp_hbm, outp, load_sem.at[2])
    load_outp.start()
    load_store = pltpu.make_async_copy(store_hbm, store, load_sem.at[3])
    load_store.start()

    load_ids.wait()
    target_col = jnp.broadcast_to(ids_ref[0].astype(jnp.float32), (LANES, tok)).T
    keep_row = ids_ref[1].astype(jnp.float32)
    keep_col = jnp.broadcast_to(keep_row, (LANES, tok)).T
    first = (v * cols).astype(jnp.float32)
    colstat[1] = target_col - first
    colstat[2] = keep_col

    load_hidden.wait()
    load_inp.wait()
    early[i, 0:rank, :] = dot_nt(inp[...], hidden[...]).astype(jnp.bfloat16)
    local_span = (ids_ref[2] - i * SPAN_DEV).astype(jnp.float32)
    early[i, rank : rank + ROWS16, :] = jnp.broadcast_to(local_span, (ROWS16, tok)).astype(
        jnp.bfloat16
    )

    for c in range(chunks):
        load_panel[c].wait()
        piece = pl.ds(c * width, width)
        logits[:, piece] = jnp.dot(hidden[...], panel[:, piece], preferred_element_type=jnp.float32)

    step = 32
    lane = lax.broadcasted_iota(jnp.int32, (step, LANES), 1)
    number = lax.broadcasted_iota(jnp.int32, (step, cols), 1).astype(jnp.float32)

    @pl.loop(0, tok // step)
    def _(r):
        at = pl.ds(pl.multiple_of(r * step, step), step)
        l = logits[at, :]
        m = jnp.max(l, axis=1, keepdims=True)
        e = jnp.exp(l - m)
        s = jnp.sum(e, axis=1, keepdims=True)
        colstat[0, at, :] = jnp.where(lane == 0, m, s)
        both[at, :] = e.astype(jnp.bfloat16)
        hit = number == colstat[1, at, 0:1]
        lower = pl.ds(pl.multiple_of(tok + r * step, step), step)
        both[lower, :] = jnp.where(hit, colstat[2, at, 0:1], 0.0).astype(jnp.bfloat16)

    mine = colstat[0].T[0:8, :]
    stat[v] = mine

    pl.semaphore_wait(barrier, n_voc + n_tok - 2)
    sends = []

    def send(copy):
        copy.start()
        sends.append(copy)

    for k, w in enumerate(vpeers):
        send(remote(stat.at[v], stat.at[v], stat_s.at[k], stat_r.at[v], i, w))
    for k, t in enumerate(tpeers):
        send(remote(early.at[i], early.at[i], early_s.at[k], early_r.at[i], t, v))

    load_outp.wait()
    outer2 = dot_nt(outp[...], both[...])

    @pl.loop(0, n_voc)
    def _(d):
        at = pl.ds(pl.multiple_of(d * out_cols, out_cols), out_cols)
        prod[d] = dot_nt(both[...], panel[at, :])

    for k, w in enumerate(vpeers):
        remote(stat.at[v], stat.at[w], stat_s.at[k], stat_r.at[w], i, w).wait_recv()
    tops = [stat[w, 0:1, :] for w in range(n_voc)]
    top = functools.reduce(jnp.maximum, tops)
    total = functools.reduce(
        jnp.add, [stat[w, 1:2, :] * jnp.exp(tops[w] - top) for w in range(n_voc)]
    )
    lse = top + jnp.log(total)
    factor = keep_row * jnp.exp(mine[0:1, :] - lse)
    colstat[3] = jnp.broadcast_to(factor, (LANES, tok)).T
    factor_col = colstat[3, :, 0:1]

    outer_t = (factor * outer2[:, :tok] - outer2[:, tok:]).astype(jnp.bfloat16)
    for j in range(n_voc):
        a, h = j // halves, j % halves
        opart[j] = outer_t[a * ROWS16 : (a + 1) * ROWS16, h * LANES : (h + 1) * LANES]
    for k, w in enumerate(vpeers):
        send(remote(opart.at[w], rs.at[v], rs_s.at[k], rs_r.at[v], i, w))

    def part_of(d):
        return factor_col * prod[d, 0:tok, :] - prod[d, tok : 2 * tok, :]

    shifts = [nz // 2] + [k for k in range(1, nz) if k != nz // 2] + [0]
    order = [lax.rem(z + k, nz) for k in shifts]

    def send_x(k):
        xsrc[k] = part_of(order[k] * PAIR + (PAIR - 1 - x)).astype(jnp.bfloat16)
        send(remote(xsrc.at[k], xdst.at[k], x_s.at[k], x_r.at[k], i, partner))

    def pass_on(k):
        zz = order[k]
        remote(xsrc.at[k], xdst.at[k], x_s.at[k], x_r.at[k], i, partner).wait_recv()
        total_k = part_of(zz * PAIR + x) + xdst[k].astype(jnp.float32)
        if k == nz - 1:
            return total_k
        zsrc[k] = total_k.astype(jnp.bfloat16)
        send(remote(zsrc.at[k], zdst.at[z], z_s.at[k], z_r.at[z], i, zz * PAIR + x))

    send_x(0)
    for k, t in enumerate(tpeers):
        remote(early.at[i], early.at[t], early_s.at[k], early_r.at[t], t, v).wait_recv()
    span_no = lax.broadcasted_iota(jnp.int32, (SPAN_DEV, tok), 0).astype(jnp.float32)

    @pl.loop(0, n_tok)
    def _(b):
        ids = early[b, rank : rank + ROWS16, :].astype(jnp.float32)[0:1]
        member = (span_no == ids).astype(jnp.float32)
        inner_t = early[b, 0:rank, :].astype(jnp.float32)
        for a in range(rank):
            weights[b, a * SPAN_DEV : (a + 1) * SPAN_DEV, :] = (
                member * inner_t[a : a + 1, :]
            ).astype(jnp.bfloat16)

    for k, w in enumerate(vpeers):
        remote(opart.at[w], rs.at[w], rs_s.at[k], rs_r.at[w], i, w).wait_recv()
    rs[v] = opart[v]
    outer_mine = functools.reduce(jnp.add, [rs[w].astype(jnp.float32) for w in range(n_voc)])
    oall[i, v] = outer_mine.astype(jnp.bfloat16)
    for k, w in enumerate(vpeers):
        send(remote(oall.at[i, v], oall.at[i, v], ag_s.at[k], ag_r.at[v], i, w))
    for k in range(1, nz):
        send_x(k)
    pass_on(0)

    for k, w in enumerate(vpeers):
        remote(oall.at[i, v], oall.at[i, w], ag_s.at[k], ag_r.at[w], i, w).wait_recv()
    for k, t in enumerate(tpeers):
        send(remote(oall.at[i], oall.at[i], late_s.at[k], late_r.at[i], t, v))
    pass_on(1)

    for k, t in enumerate(tpeers):
        remote(oall.at[i], oall.at[t], late_s.at[k], late_r.at[t], t, v).wait_recv()
    low = lax.broadcasted_iota(jnp.int32, (SPAN_DEV, LANES), 1) < rank

    @pl.loop(0, n_tok)
    def _(b):
        rows = []
        for a in range(rank // ROWS16):
            rows.append(
                jnp.concatenate([oall[b, a * halves + h] for h in range(halves)], axis=1)
            )
        outer_b = jnp.concatenate(rows * (LANES // rank), axis=0)
        sums = dot_nt(weights[b], outer_b)
        at = pl.ds(pl.multiple_of(b * SPAN_DEV, SPAN_DEV), SPAN_DEV)
        for a in range(0, rank, 2):
            even = sums[a * SPAN_DEV : (a + 1) * SPAN_DEV]
            odd = sums[(a + 1) * SPAN_DEV : (a + 2) * SPAN_DEV]
            queries[at, a * rank : (a + 2) * rank] = jnp.where(low, even, odd).astype(
                jnp.bfloat16
            )

    for k in range(2, nz - 1):
        pass_on(k)
    load_store.wait()
    scores_ref[...] = dot_nt(queries[...], store[...]) / rank

    kept = pass_on(nz - 1)
    for k in range(1, nz):
        w = lax.rem(z + k, nz)
        remote(zsrc.at[0], zdst.at[w], z_s.at[0], z_r.at[w], i, w * PAIR + x).wait_recv()
    zdst[z] = jnp.zeros_like(zdst[z])
    hg_ref[...] = (
        kept
        + functools.reduce(jnp.add, [zdst[w].astype(jnp.float32) for w in range(nz)])
    ).astype(jnp.bfloat16)
    for copy in sends:
        copy.wait_send()


def fused_fits(n_tok, n_voc, hidden, panel, in_proj):
    tok, dim = hidden.shape
    rank = in_proj.shape[1]
    return (
        n_voc % PAIR == 0
        and n_voc // PAIR > 2
        and n_tok > 1
        and (rank // ROWS16) * (tok // LANES) == n_voc
        and rank * 2 == LANES
        and dim % (n_voc * LANES) == 0
        and panel.shape[1] % (2 * LANES) == 0
        and SPAN_DEV % ROWS16 == 0
    )


def body(n_tok, n_voc, hidden, panel, in_proj, out_proj, targets, keep, span_ids, store):
    if not fused_fits(n_tok, n_voc, hidden, panel, in_proj):
        return plain_body(hidden, panel, in_proj, out_proj, targets, keep, span_ids, store)
    tok, dim = hidden.shape
    cols = panel.shape[1]
    rank = in_proj.shape[1]
    out_cols = dim // n_voc
    nz = n_voc // PAIR
    chunks = cols // (2 * LANES)
    bf, f32 = jnp.bfloat16, jnp.float32
    block = (nz, tok, out_cols)
    dma = pltpu.SemaphoreType.DMA
    anywhere = pl.BlockSpec(memory_space=pltpu.HBM)
    vmem = pl.BlockSpec(memory_space=pltpu.VMEM)
    return pl.pallas_call(
        functools.partial(fused_kernel, n_tok, n_voc, chunks),
        out_shape=(
            jax.ShapeDtypeStruct((tok, out_cols), bf),
            jax.ShapeDtypeStruct((n_tok * SPAN_DEV, store.shape[0]), f32),
        ),
        in_specs=[anywhere] * 6,
        out_specs=(vmem, vmem),
        scratch_shapes=[
            pltpu.VMEM(hidden.shape, bf),
            pltpu.VMEM(panel.shape, bf),
            pltpu.VMEM((rank, dim), bf),
            pltpu.VMEM((rank, cols), bf),
            pltpu.VMEM(store.shape, bf),
            pltpu.VMEM((3, 1, tok), jnp.int32),
            pltpu.VMEM((tok, cols), f32),
            pltpu.VMEM((4, tok, LANES), f32),
            pltpu.VMEM((2 * tok, cols), bf),
            pltpu.VMEM((n_voc, 2 * tok, out_cols), f32),
            pltpu.VMEM((n_voc, 8, tok), f32),
            pltpu.VMEM((n_tok, rank + ROWS16, tok), bf),
            pltpu.VMEM((n_voc, ROWS16, LANES), bf),
            pltpu.VMEM((n_voc, ROWS16, LANES), bf),
            pltpu.VMEM((n_tok, n_voc, ROWS16, LANES), bf),
            pltpu.VMEM((n_tok, rank * SPAN_DEV, tok), bf),
            pltpu.VMEM((n_tok * SPAN_DEV, rank * rank), bf),
            pltpu.VMEM(block, bf),
            pltpu.VMEM(block, bf),
            pltpu.VMEM(block, bf),
            pltpu.VMEM(block, bf),
            dma((5,)),
            dma((chunks,)),
            dma((n_voc,)),
            dma((n_voc,)),
            dma((n_tok,)),
            dma((n_tok,)),
            dma((n_voc,)),
            dma((n_voc,)),
            dma((n_voc,)),
            dma((n_voc,)),
            dma((n_tok,)),
            dma((n_tok,)),
            dma((nz,)),
            dma((nz,)),
            dma((nz,)),
            dma((nz,)),
        ],
        compiler_params=pltpu.CompilerParams(
            collective_id=0, has_side_effects=True, vmem_limit_bytes=54900 * 1024
        ),
    )(
        hidden,
        panel,
        in_proj.T,
        out_proj.T,
        jnp.stack([targets, keep, span_ids]).reshape(3, 1, tok),
        store,
    )


def solution(mesh):
    placed = (
        P("tok", None),
        P(None, "voc"),
        P(),
        P("voc", None),
        P("tok"),
        P("tok"),
        P("tok"),
        P(("tok", "voc"), None),
    )
    return jax.shard_map(
        functools.partial(body, mesh.shape["tok"], mesh.shape["voc"]),
        mesh=mesh,
        in_specs=placed,
        out_specs=(P("tok", "voc"), P(None, ("tok", "voc"))),
        check_vma=False,
    )
```
